128 devices in a mesh: fsdp: 8 (over y, x_lo), row: 4 (over x_hi, core), col: 4 (over z).
Axes of the slice: x: 4 (x_hi: 2, x_lo: 2; x = x_hi * 2 + x_lo), y: 4, z: 4, core: 2. Of those that a mesh axis runs over, the one named last changes fastest.
Arguments:
- grad: bfloat16 [8, 1024, 16384], P(None, 'fsdp', ('row', 'col')), may hold values from -6 to 6
- momentum: float32 [8, 1024, 16384], P(None, 'fsdp', ('row', 'col')), may hold values from -6 to 6
- variance: float32 [8, 1024, 16384], P(None, 'fsdp', ('row', 'col')), may hold values from 0.05 to 4
- weight: bfloat16 [8, 1024, 16384], P(None, 'fsdp', ('row', 'col')), may hold values from -6 to 6
- left_inverse: float32 [8, 1024, 1024], P('row', ('fsdp', 'col')), may hold values from -1 to 4, as said below
- right_inverse: float32 [4, 4, 1024, 1024], P(None, 'col', ('fsdp', 'row')), may hold values from -1 to 4, as said below
Outputs:
- momentum_next: float32 [8, 1024, 16384], P(None, 'fsdp', ('row', 'col'))
- variance_next: float32 [8, 1024, 16384], P(None, 'fsdp', ('row', 'col'))
- weight_next: bfloat16 [8, 1024, 16384], P(None, 'fsdp', ('row', 'col'))
The draws below stay inside these ranges and needn't reach their ends.
Inputs may be any that keep to these rules, and one draw needn't show every extreme that they name: `left_inverse`: each block is symmetric positive definite. `right_inverse`: each block is symmetric positive definite.
All inputs are finite; a program needn't handle non-finite values.
Results may differ from the reference program's by a relative error of at most 0.001.
Values sent between devices are 32-bit elements; how exact they have to be, the bound alone decides.
A program may use at most 128 MiB of HBM per device.

```python
import math
import jax
import jax.numpy as jnp
from jax import lax

B = 1024
COLS = 16384
RB = 8
CB = 16
N_COL = 4


def definite_blocks(key, count):
    diag_key, noise_key = jax.random.split(key)
    diagonal = jax.random.uniform(diag_key, (count, B), jnp.float32, 1.0, 2.0)
    noise = jax.random.truncated_normal(noise_key, -4.0, 4.0, (count, B, B), jnp.float32) * (0.35 / math.sqrt(B))
    sym_part = (noise + jnp.swapaxes(noise, 1, 2)) / math.sqrt(2.0)
    return sym_part + diagonal[:, :, None] * jnp.eye(B, dtype=jnp.float32)[None]


def draw_left_inverse(key, part):
    return definite_blocks(jax.random.fold_in(key, 11), RB)


def draw_right_inverse(key, part):
    return definite_blocks(jax.random.fold_in(key, 23), CB).reshape(CB // N_COL, N_COL, B, B)


def block_scale(stream_key, shape, pieces, low, largest):
    factor_of, own = 1.0, jax.random.fold_in(stream_key, 6)
    for axis_at, blocks in pieces:
        draws = jnp.exp(jax.random.uniform(jax.random.fold_in(own, axis_at), (blocks,), jnp.float32, low / len(pieces), largest / len(pieces)))
        factor_of = factor_of * jnp.repeat(draws, shape[axis_at] // blocks).reshape([-1 if axis == axis_at else 1 for axis in range(len(shape))])
    return factor_of


def bell_draw(key, shape, width, limit, pieces=(), held_as=jnp.bfloat16):
    drawn = jax.random.normal(key, shape, jnp.float32) * width
    if len(pieces) > 0:
        drawn = block_scale(key, shape, pieces, -0.22, 0.18) * drawn
    return jnp.clip(drawn, min=-limit, max=limit).astype(held_as)


def setup_inputs(seed: int = 0) -> dict:
    key_list = jax.random.split(jax.random.key(seed), 7)
    grad = bell_draw(key_list[0], (RB, B, COLS), 1.0, 6.0, ((1, 8), (2, 16)))
    momentum = bell_draw(key_list[1], (RB, B, COLS), 1.0, 6.0, ((1, 8), (2, 16)), jnp.float32)
    variance = jnp.clip(jnp.exp(math.log(4.0) - 4.3820266 * jax.random.uniform(key_list[2], (RB, B, COLS), jnp.float32) ** block_scale(key_list[2], (RB, B, COLS), ((1, 8), (2, 16)), -0.2, 0.2)), 0.05, 4.0)
    weight = bell_draw(key_list[3], (RB, B, COLS), 1.0, 6.0, ((1, 8), (2, 16)))
    left_inverse = draw_left_inverse(jax.random.fold_in(key_list[6], 71), 0)
    right_inverse = draw_right_inverse(jax.random.fold_in(key_list[6], 71), 0)
    return {"grad": grad, "momentum": momentum, "variance": variance, "weight": weight, "left_inverse": left_inverse, "right_inverse": right_inverse}


def precondition(momentum_next, left_inverse, right_inverse):
    right_blocks = right_inverse.reshape(CB, B, B).astype(jnp.float32)

    def one_block(pair):
        left_block, rows = pair
        mixed = jnp.dot(left_block, rows, precision=lax.Precision.HIGHEST, preferred_element_type=jnp.float32)
        parted = mixed.reshape(B, CB, B)
        joined = jnp.einsum('icp,cpn->icn', parted, right_blocks, precision=lax.Precision.HIGHEST)
        return joined.reshape(B, COLS)
    return lax.map(one_block, (left_inverse, momentum_next))

def reference(grad, momentum, variance, weight, left_inverse, right_inverse):
    momentum_next = 0.9 * momentum + 0.1 * grad.astype(jnp.float32)
    precond = precondition(momentum_next, left_inverse, right_inverse)
    variance_next = 0.95 * variance + 0.05 * precond * precond
    weight_float = weight.astype(jnp.float32)
    weight_next = weight_float - 0.1 * (precond / (jnp.sqrt(variance_next) + 1e-08) + 0.1 * weight_float)
    return (momentum_next, variance_next, weight_next.astype(jnp.bfloat16))
```

```python
import functools

import jax
import jax.numpy as jnp
from jax import lax
from jax.experimental import pallas as pl
from jax.experimental.pallas import tpu as pltpu
from jax.sharding import Mesh
from jax.sharding import PartitionSpec as P

AXES = ("y", "a", "h", "k", "z")
MESH = pl.DeviceIdType.MESH

first_decay = 0.9
second_decay = 0.95
learn_rate = 0.1
weight_decay = 0.1
epsilon = 1e-08

PARTS = 4
WIDE = 1024 // PARTS


def split(x):
    high = x.astype(jnp.bfloat16)
    low = (x - high.astype(jnp.float32)).astype(jnp.bfloat16)
    return high, low


def product(left_high, left_low, right_high, right_low):
    dot = functools.partial(jnp.dot, preferred_element_type=jnp.float32)
    return dot(left_high, right_high) + (dot(left_high, right_low) + dot(left_low, right_high))


def kernel(
    grad, momentum, left, right, out,
    grad_in, own, tile, left_all, right_all, left_hi, left_lo, right_hi, right_lo,
    tile_hi, tile_lo, mixed_hi, mixed_lo, done,
    in_sem, own_send, own_recv, l1_send, l1_recv, l2_send, l2_recv, l3_send, l3_recv,
    r1_send, r1_recv, r2_send, r2_recv, r3_send, r3_recv, p_send, p_recv,
):
    y, a, h, k, z = (lax.axis_index(name) for name in AXES)
    me_f = 2 * y + a

    def remote(src, dst, send, recv, device):
        return pltpu.make_async_remote_copy(
            src_ref=src, dst_ref=dst, send_sem=send, recv_sem=recv, device_id=device, device_id_type=MESH
        )

    def arrived(dst, recv):
        pltpu.make_async_copy(dst, dst, recv).wait()

    loads = []
    for b in range(8):
        pair = (
            pltpu.make_async_copy(momentum.at[b], own.at[b], in_sem.at[0, b]),
            pltpu.make_async_copy(grad.at[b], grad_in.at[b], in_sem.at[1, b]),
        )
        for copy in pair:
            copy.start()
        loads.append(pair)

    barrier = pltpu.get_barrier_semaphore()
    others = []
    for dy in range(4):
        for da in range(2):
            for dk in range(2):
                if (dy, da, dk) != (0, 0, 0):
                    others.append((lax.rem(y + dy, 4), lax.rem(a + da, 2), h, lax.rem(k + dk, 2), z))
    for da in range(2):
        others.append((y, lax.rem(a + da, 2), 1 - h, k, z))
    for dz in range(1, 4):
        others.append((y, a, h, k, lax.rem(z + dz, 4)))
    for device in others:
        pl.semaphore_signal(barrier, inc=1, device_id=device, device_id_type=MESH)
    pl.semaphore_wait(barrier, len(others))

    home = 2 * h + k
    holder = h == y // 2
    for t in range(2):
        stays = jnp.logical_and(y == home, k == t)

        @pl.when(stays)
        def _():
            pltpu.make_async_copy(left.at[t], left_all.at[y, a, z], l1_recv.at[y]).start()

        @pl.when(jnp.logical_not(stays))
        def _():
            remote(
                left.at[t], left_all.at[y, a, z], l1_send.at[t], l1_recv.at[y], (home, a, h, jnp.int32(t), z)
            ).start()

    def r1(i):
        to_a, to_h = lax.rem(a + i % 2, 2), lax.rem(h + i // 2, 2)
        return remote(
            right.at[2 * to_h + to_a, 0], right_all.at[y, a, h, k], r1_send.at[i], r1_recv.at[i], (y, to_a, to_h, k, z)
        )

    pltpu.make_async_copy(right.at[2 * h + a, 0], right_all.at[y, a, h, k], r1_recv.at[0]).start()
    for i in range(1, 4):
        r1(i).start()

    def own_part(dy, t, part):
        to_y = lax.rem(y + dy, 4)
        columns = pl.ds(part * WIDE, WIDE)
        return (
            own.at[2 * to_y + t, :, columns],
            tile.at[me_f, :, columns],
            own_send.at[dy, t, part],
            own_recv.at[me_f, part],
            (to_y, k, h, jnp.int32(t), z),
        )

    for b in range(8):
        for copy in loads[b]:
            copy.wait()
        own[b] = first_decay * own[b] + (1.0 - first_decay) * grad_in[b].astype(jnp.float32)
    for part in range(PARTS):
        for dy in (2, 1, 3, 0):
            for t in range(2):
                src, dst, send, recv, device = own_part(dy, t, part)
                if dy == 0:
                    stays = jnp.logical_and(a == k, k == t)

                    @pl.when(stays)
                    def _():
                        pltpu.make_async_copy(src, dst, recv).start()

                    @pl.when(jnp.logical_not(stays))
                    def _():
                        remote(src, dst, send, recv, device).start()
                else:
                    remote(src, dst, send, recv, device).start()

    for i in range(4):
        arrived(right_all.at[y, lax.rem(a + i % 2, 2), lax.rem(h + i // 2, 2), k], r1_recv.at[i])

    def r2(dy):
        rows = right_all.at[y, :, :, k]
        return remote(rows, rows, r2_send.at[dy - 1], r2_recv.at[dy - 1], (lax.rem(y + dy, 4), a, h, k, z))

    def r3(dy):
        rows = right_all.at[lax.rem(y - dy + 4, 4), :, :, k]
        return remote(rows, rows, r3_send.at[dy], r3_recv.at[dy], (y, a, h, 1 - k, z))

    for dy in (2, 1, 3):
        r2(dy).start()
    r3(0).start()

    def l2(i):
        rows = left_all.at[:, a, z]
        device = (y, lax.rem(a + i % 2, 2), lax.rem(h + i // 2, 2), k, z)
        return remote(rows, rows, l2_send.at[i - 1], l2_recv.at[a], device)

    @pl.when(holder)
    def _():
        for from_y in range(4):
            arrived(left_all.at[from_y, a, z], l1_recv.at[from_y])
        for i in range(1, 4):
            l2(i).start()

    def l3(i, dz):
        rows = left_all.at[:, lax.rem(a + i, 2), z]
        return remote(rows, rows, l3_send.at[i, dz - 1], l3_recv.at[lax.rem(a + i, 2), dz - 1],
                      (y, a, h, k, lax.rem(z + dz, 4)))

    for i in range(2):
        from_a = lax.rem(a + i, 2)
        if i == 0:

            @pl.when(jnp.logical_not(holder))
            def _():
                arrived(left_all.at[:, from_a, z], l2_recv.at[from_a])
        else:
            arrived(left_all.at[:, from_a, z], l2_recv.at[from_a])
        for dz in (2, 1, 3):
            l3(i, dz).start()

    for dy in (1, 3, 2):
        from_y = lax.rem(y - dy + 4, 4)
        arrived(right_all.at[from_y, :, :, k], r2_recv.at[dy - 1])
        r3(dy).start()

    def split_left(from_z):
        for f in range(8):
            high, low = split(left_all[f // 2, f % 2, from_z])
            rows = pl.ds(pl.multiple_of(f * 128 + from_z * 32, 32), 32)
            left_hi[rows], left_lo[rows] = high, low

    split_left(z)
    for dz in (1, 3, 2):
        from_z = lax.rem(z - dz + 4, 4)
        for from_a in range(2):
            arrived(left_all.at[:, from_a, from_z], l3_recv.at[from_a, dz - 1])
        split_left(from_z)

    for part in range(PARTS):
        columns = slice(part * WIDE, (part + 1) * WIDE)
        for f in range(8):
            arrived(tile.at[f, :, columns], own_recv.at[f, part])

        @pl.loop(0, 8)
        def _(f):
            rows = pl.ds(pl.multiple_of(f * 128, 128), 128)
            tile_hi[rows], tile_lo[rows] = split(tile[f, :, columns])

        @pl.loop(0, 4)
        def _(i):
            rows = pl.ds(pl.multiple_of(i * 256, 256), 256)
            mixed = product(left_hi[rows], left_lo[rows], tile_hi[...], tile_lo[...])
            mixed_hi[rows, columns], mixed_lo[rows, columns] = split(mixed)

    for dy in (0, 1, 3, 2):
        arrived(right_all.at[lax.rem(y - dy + 4, 4), :, :, 1 - k], r3_recv.at[dy])

    @pl.loop(0, 32)
    def _(i):
        rows = pl.ds(pl.multiple_of(i * 32, 32), 32)
        right_hi[rows], right_lo[rows] = split(right_all[i // 8, (i // 4) % 2, (i // 2) % 2, i % 2])

    def p_copy(dy, to_a):
        to_y = lax.rem(y + dy, 4)
        return (done.at[2 * to_y + to_a], out.at[2 * y + k], p_send.at[dy, to_a], p_recv.at[2 * y + k],
                (to_y, jnp.int32(to_a), h, a, z))

    for dy in (2, 1, 3, 0):
        to_y = lax.rem(y + dy, 4)
        rows = pl.ds(pl.multiple_of(to_y * 256, 256), 256)

        @pl.loop(0, 4)
        def _(i):
            columns = pl.ds(pl.multiple_of(i * 256, 256), 256)
            both = product(mixed_hi[rows], mixed_lo[rows], right_hi[:, columns], right_lo[:, columns])
            done[2 * to_y, :, columns] = both[:128]
            done[2 * to_y + 1, :, columns] = both[128:]

        for to_a in range(2):
            src, dst, send, recv, device = p_copy(dy, to_a)
            if dy == 0:
                stays = jnp.logical_and(a == k, a == to_a)

                @pl.when(stays)
                def _():
                    pltpu.make_async_copy(src, dst, recv).start()

                @pl.when(jnp.logical_not(stays))
                def _():
                    remote(src, dst, send, recv, device).start()
            else:
                remote(src, dst, send, recv, device).start()

    for t in range(2):

        @pl.when(jnp.logical_not(jnp.logical_and(y == home, k == t)))
        def _():
            remote(
                left.at[t], left_all.at[y, a, z], l1_send.at[t], l1_recv.at[y], (home, a, h, jnp.int32(t), z)
            ).wait_send()

    for i in range(1, 4):
        r1(i).wait_send()

    @pl.when(holder)
    def _():
        for i in range(1, 4):
            l2(i).wait_send()

    for i in range(2):
        for dz in range(1, 4):
            l3(i, dz).wait_send()
    for dy in range(1, 4):
        r2(dy).wait_send()
    for dy in range(4):
        r3(dy).wait_send()
    for dy in range(4):
        for t in range(2):
            sends = [remote(*own_part(dy, t, part)) for part in range(PARTS)] + [remote(*p_copy(dy, t))]
            if dy == 0:

                @pl.when(jnp.logical_not(jnp.logical_and(a == k, k == t)))
                def _():
                    for copy in sends:
                        copy.wait_send()
            else:
                for copy in sends:
                    copy.wait_send()
    for b in range(8):
        arrived(out.at[b], p_recv.at[b])


def precondition(grad, momentum, left, right):
    f32, bf16 = jnp.float32, jnp.bfloat16
    dma = pltpu.SemaphoreType.DMA
    return pl.pallas_call(
        kernel,
        out_shape=jax.ShapeDtypeStruct((8, 128, 1024), f32),
        in_specs=[pl.BlockSpec(memory_space=pl.ANY)] * 4,
        out_specs=pl.BlockSpec(memory_space=pl.ANY),
        scratch_shapes=[
            pltpu.VMEM((8, 128, 1024), bf16),
            pltpu.VMEM((8, 128, 1024), f32),
            pltpu.VMEM((8, 128, 1024), f32),
            pltpu.VMEM((4, 2, 4, 32, 1024), f32),
            pltpu.VMEM((4, 2, 2, 2, 32, 1024), f32),
            pltpu.VMEM((1024, 1024), bf16),
            pltpu.VMEM((1024, 1024), bf16),
            pltpu.VMEM((1024, 1024), bf16),
            pltpu.VMEM((1024, 1024), bf16),
            pltpu.VMEM((1024, WIDE), bf16),
            pltpu.VMEM((1024, WIDE), bf16),
            pltpu.VMEM((1024, 1024), bf16),
            pltpu.VMEM((1024, 1024), bf16),
            pltpu.VMEM((8, 128, 1024), f32),
            dma((2, 8)),
            dma((4, 2, PARTS)), dma((8, PARTS)),
            dma((2,)), dma((4,)), dma((3,)), dma((2,)), dma((2, 3)), dma((2, 3)),
            dma((4,)), dma((4,)), dma((3,)), dma((3,)), dma((4,)), dma((4,)),
            dma((4, 2)), dma((8,)),
        ],
        compiler_params=pltpu.CompilerParams(
            collective_id=0, has_side_effects=True, vmem_limit_bytes=56 * 2**20
        ),
        cost_estimate=pl.CostEstimate(flops=3 * 2**32, bytes_accessed=20 * 2**20, transcendentals=0),
    )(grad, momentum, left, right)


def per_device(grad, momentum, variance, weight, left_inverse, right_inverse):
    precond = precondition(grad, momentum, left_inverse, right_inverse)
    momentum_next = first_decay * momentum + (1.0 - first_decay) * grad.astype(jnp.float32)
    variance_next = second_decay * variance + (1.0 - second_decay) * precond * precond
    weight_float = weight.astype(jnp.float32)
    weight_next = weight_float - learn_rate * (
        precond / (jnp.sqrt(variance_next) + epsilon) + weight_decay * weight_float
    )
    return (momentum_next, variance_next, weight_next.astype(jnp.bfloat16))


def solution(mesh):
    torus = Mesh(mesh.devices.reshape(4, 2, 2, 2, 4), AXES)
    tiles = P(None, ("y", "a"), ("h", "k", "z"))
    in_specs = (
        tiles,
        tiles,
        tiles,
        tiles,
        P(("h", "k"), ("y", "a", "z"), None),
        P(None, "z", ("y", "a", "h", "k"), None),
    )
    return jax.shard_map(
        per_device, mesh=torus, in_specs=in_specs, out_specs=(tiles, tiles, tiles), check_vma=False
    )
```

```python
import functools

import jax
import jax.numpy as jnp
from jax import lax
from jax.experimental import pallas as pl
from jax.experimental.pallas import tpu as pltpu
from jax.sharding import Mesh
from jax.sharding import PartitionSpec as P

AXES = ("y", "a", "h", "k", "z")
MESH = pl.DeviceIdType.MESH

first_decay = 0.9
second_decay = 0.95
learn_rate = 0.1
weight_decay = 0.1
epsilon = 1e-08

PARTS = 4
WIDE = 1024 // PARTS
KEPT = 5


def split(x):
    high = x.astype(jnp.bfloat16)
    low = (x - high.astype(jnp.float32)).astype(jnp.bfloat16)
    return high, low


def product(left_high, left_low, right_high, right_low):
    dot = functools.partial(jnp.dot, preferred_element_type=jnp.float32)
    return dot(left_high, right_high) + (dot(left_high, right_low) + dot(left_low, right_high))


def kernel(
    grad, momentum, left, right, out,
    grad_in, own, tile, left_own, right_own, left_all, right_all, left_hi, left_lo, right_hi, right_lo,
    tile_hi, tile_lo, mixed_hi, mixed_lo, done,
    in_sem, pack_sem, own_send, own_recv, l1_send, l1_recv, l2_send, l2_recv, l3_send, l3_recv, l4_send, l4_recv,
    r1_send, r1_recv, r2_send, r2_recv, r3_send, r3_recv, r4_send, r4_recv, p_send, p_recv,
):
    y, a, h, k, z = (lax.axis_index(name) for name in AXES)
    me_f = 2 * y + a

    def step(at, by):
        return lax.rem(at + by + 4, 4)

    def remote(src, dst, send, recv, device):
        return pltpu.make_async_remote_copy(
            src_ref=src, dst_ref=dst, send_sem=send, recv_sem=recv, device_id=device, device_id_type=MESH
        )

    def arrived(dst, recv):
        pltpu.make_async_copy(dst, dst, recv).wait()

    packs = []
    for d in range(KEPT):
        columns = pl.ds(pl.multiple_of(lax.rem(me_f + d, 8) * 128, 128), 128)
        packed = pl.ds(d * 128, 128)
        packs.append(pltpu.make_async_copy(left.at[:, :, columns], left_own.at[:, :, packed], pack_sem.at[0, d]))
        packs.append(pltpu.make_async_copy(right.at[:, 0, :, columns], right_own.at[:, :, packed], pack_sem.at[1, d]))
    for copy in packs:
        copy.start()
    loads = []
    for b in range(8):
        pair = (
            pltpu.make_async_copy(momentum.at[b], own.at[b], in_sem.at[0, b]),
            pltpu.make_async_copy(grad.at[b], grad_in.at[b], in_sem.at[1, b]),
        )
        for copy in pair:
            copy.start()
        loads.append(pair)

    barrier = pltpu.get_barrier_semaphore()
    others = []
    for dy in range(4):
        for da in range(2):
            for dk in range(2):
                if (dy, da, dk) != (0, 0, 0):
                    others.append((step(y, dy), lax.rem(a + da, 2), h, lax.rem(k + dk, 2), z))
    for da in range(2):
        others.append((y, lax.rem(a + da, 2), 1 - h, k, z))
    for dz in range(1, 4):
        others.append((y, a, h, k, step(z, dz)))
    for device in others:
        pl.semaphore_signal(barrier, inc=1, device_id=device, device_id_type=MESH)
    for copy in packs:
        copy.wait()
    pl.semaphore_wait(barrier, len(others))

    home = 2 * h + k
    holder = h == y // 2

    def l1(t):
        return remote(
            left_own.at[t], left_all.at[y, a, z], l1_send.at[t], l1_recv.at[y], (home, a, h, jnp.int32(t), z)
        )

    for t in range(2):
        stays = jnp.logical_and(y == home, k == t)

        @pl.when(stays)
        def _():
            pltpu.make_async_copy(left_own.at[t], left_all.at[y, a, z], l1_recv.at[y]).start()

        @pl.when(jnp.logical_not(stays))
        def _():
            l1(t).start()

    def r1(i):
        to_a, to_h = lax.rem(a + i % 2, 2), lax.rem(h + i // 2, 2)
        return remote(
            right_own.at[2 * to_h + to_a], right_all.at[y, a, h, k], r1_send.at[i], r1_recv.at[i], (y, to_a, to_h, k, z)
        )

    pltpu.make_async_copy(right_own.at[2 * h + a], right_all.at[y, a, h, k], r1_recv.at[0]).start()
    for i in range(1, 4):
        r1(i).start()

    def own_part(dy, t, part):
        to_y = step(y, dy)
        columns = pl.ds(part * WIDE, WIDE)
        return (
            own.at[2 * to_y + t, :, columns],
            tile.at[me_f, :, columns],
            own_send.at[dy, t, part],
            own_recv.at[me_f, part],
            (to_y, k, h, jnp.int32(t), z),
        )

    def send_part(part):
        for dy in (2, 1, 3, 0):
            for t in range(2):
                src, dst, send, recv, device = own_part(dy, t, part)
                if dy == 0:
                    stays = jnp.logical_and(a == k, k == t)

                    @pl.when(stays)
                    def _():
                        pltpu.make_async_copy(src, dst, recv).start()

                    @pl.when(jnp.logical_not(stays))
                    def _():
                        remote(src, dst, send, recv, device).start()
                else:
                    remote(src, dst, send, recv, device).start()

    for b in range(8):
        for copy in loads[b]:
            copy.wait()
        own[b] = first_decay * own[b] + (1.0 - first_decay) * grad_in[b].astype(jnp.float32)
    send_part(0)

    def l2(i):
        rows = left_all.at[:, a, z]
        device = (y, lax.rem(a + i % 2, 2), lax.rem(h + i // 2, 2), k, z)
        return remote(rows, rows, l2_send.at[i - 1], l2_recv.at[a], device)

    @pl.when(holder)
    def _():
        for from_y in range(4):
            arrived(left_all.at[from_y, a, z], l1_recv.at[from_y])
        for i in (2, 3, 1):
            l2(i).start()

    def r2(s):
        rows = right_all.at[y, :, :, k]
        return remote(rows, rows, r2_send.at[s], r2_recv.at[s], (step(y, 1 - 2 * s), a, h, k, z))

    def r3(dy):
        rows = right_all.at[step(y, -dy), :, :, k]
        return remote(rows, rows, r3_send.at[dy], r3_recv.at[dy], (y, a, h, 1 - k, z))

    def r4(s):
        rows = right_all.at[step(y, 2 * s - 1), s, :, k]
        return remote(rows, rows, r4_send.at[s], r4_recv.at[s], (step(y, 1 - 2 * s), a, h, k, z))

    for i in range(4):
        arrived(right_all.at[y, lax.rem(a + i % 2, 2), lax.rem(h + i // 2, 2), k], r1_recv.at[i])
    for s in range(2):
        r2(s).start()
    r3(0).start()
    for part in range(1, PARTS):
        send_part(part)

    def l3(i, s):
        from_a = lax.rem(a + i, 2)
        rows = left_all.at[:, from_a, z]
        return remote(rows, rows, l3_send.at[i, s], l3_recv.at[from_a, s], (y, a, h, k, step(z, 1 - 2 * s)))

    def l4(s):
        rows = left_all.at[:, s, step(z, 2 * s - 1)]
        return remote(rows, rows, l4_send.at[s], l4_recv.at[s], (y, a, h, k, step(z, 1 - 2 * s)))

    for i in range(2):
        from_a = lax.rem(a + i, 2)
        if i == 0:

            @pl.when(jnp.logical_not(holder))
            def _():
                arrived(left_all.at[:, from_a, z], l2_recv.at[from_a])
        else:
            arrived(left_all.at[:, from_a, z], l2_recv.at[from_a])
        for s in range(2):
            l3(i, s).start()

    for s in range(2):
        arrived(right_all.at[step(y, 2 * s - 1), :, :, k], r2_recv.at[s])
        r4(s).start()
        r3(1 + 2 * s).start()
    for s in range(2):
        arrived(left_all.at[:, s, step(z, 2 * s - 1)], l3_recv.at[s, s])
        l4(s).start()
    for s in range(2):
        arrived(right_all.at[step(y, 2), s, :, k], r4_recv.at[s])
    r3(2).start()
    for s in range(2):
        arrived(left_all.at[:, 1 - s, step(z, 2 * s - 1)], l3_recv.at[1 - s, s])
        arrived(left_all.at[:, s, step(z, 2)], l4_recv.at[s])

    def unpack(rows_of, high, low):
        @pl.loop(0, 8)
        def _(f):
            at = pl.ds(pl.multiple_of(f * 128, 128), 128)
            for d in range(KEPT):
                block = rows_of(f, pl.ds(d * 128, 128)).reshape(128, 128)
                to = pl.ds(pl.multiple_of(lax.rem(f + d, 8) * 128, 128), 128)
                high[at, to], low[at, to] = split(block)
                if 0 < d < 4:
                    high[to, at], low[to, at] = split(block.T)

    unpack(lambda f, c: left_all[f // 2, lax.rem(f, 2), :, :, c], left_hi, left_lo)

    for part in range(PARTS):
        columns = slice(part * WIDE, (part + 1) * WIDE)
        for f in range(8):
            arrived(tile.at[f, :, columns], own_recv.at[f, part])

        @pl.loop(0, 8)
        def _(f):
            rows = pl.ds(pl.multiple_of(f * 128, 128), 128)
            tile_hi[rows], tile_lo[rows] = split(tile[f, :, columns])

        @pl.loop(0, 4)
        def _(i):
            rows = pl.ds(pl.multiple_of(i * 256, 256), 256)
            mixed = product(left_hi[rows], left_lo[rows], tile_hi[...], tile_lo[...])
            mixed_hi[rows, columns], mixed_lo[rows, columns] = split(mixed)

        if part == max(PARTS - 2, 0):
            for dy in (0, 1, 3, 2):
                arrived(right_all.at[step(y, -dy), :, :, 1 - k], r3_recv.at[dy])
            unpack(lambda f, c: right_all[f // 2, lax.rem(f, 2), :, :, :, c], right_hi, right_lo)

    def p_copy(dy, to_a):
        to_y = step(y, dy)
        return (done.at[2 * to_y + to_a], out.at[2 * y + k], p_send.at[dy, to_a], p_recv.at[2 * y + k],
                (to_y, jnp.int32(to_a), h, a, z))

    for dy in (2, 1, 3, 0):
        to_y = step(y, dy)
        rows = pl.ds(pl.multiple_of(to_y * 256, 256), 256)

        @pl.loop(0, 4)
        def _(i):
            columns = pl.ds(pl.multiple_of(i * 256, 256), 256)
            both = product(mixed_hi[rows], mixed_lo[rows], right_hi[:, columns], right_lo[:, columns])
            done[2 * to_y, :, columns] = both[:128]
            done[2 * to_y + 1, :, columns] = both[128:]

        for to_a in range(2):
            src, dst, send, recv, device = p_copy(dy, to_a)
            if dy == 0:
                stays = jnp.logical_and(a == k, a == to_a)

                @pl.when(stays)
                def _():
                    pltpu.make_async_copy(src, dst, recv).start()

                @pl.when(jnp.logical_not(stays))
                def _():
                    remote(src, dst, send, recv, device).start()
            else:
                remote(src, dst, send, recv, device).start()

    for t in range(2):

        @pl.when(jnp.logical_not(jnp.logical_and(y == home, k == t)))
        def _():
            l1(t).wait_send()

    for i in range(1, 4):
        r1(i).wait_send()

    @pl.when(holder)
    def _():
        for i in range(1, 4):
            l2(i).wait_send()

    for s in range(2):
        l3(0, s).wait_send()
        l3(1, s).wait_send()
        l4(s).wait_send()
        r2(s).wait_send()
        r4(s).wait_send()
    for dy in range(4):
        r3(dy).wait_send()
    for dy in range(4):
        for t in range(2):
            sends = [remote(*own_part(dy, t, part)) for part in range(PARTS)] + [remote(*p_copy(dy, t))]
            if dy == 0:

                @pl.when(jnp.logical_not(jnp.logical_and(a == k, k == t)))
                def _():
                    for copy in sends:
                        copy.wait_send()
            else:
                for copy in sends:
                    copy.wait_send()
    for b in range(8):
        arrived(out.at[b], p_recv.at[b])


def precondition(grad, momentum, left, right):
    f32, bf16 = jnp.float32, jnp.bfloat16
    dma = pltpu.SemaphoreType.DMA
    return pl.pallas_call(
        kernel,
        out_shape=jax.ShapeDtypeStruct((8, 128, 1024), f32),
        in_specs=[pl.BlockSpec(memory_space=pl.ANY)] * 4,
        out_specs=pl.BlockSpec(memory_space=pl.ANY),
        scratch_shapes=[
            pltpu.VMEM((8, 128, 1024), bf16),
            pltpu.VMEM((8, 128, 1024), f32),
            pltpu.VMEM((8, 128, 1024), f32),
            pltpu.VMEM((2, 32, KEPT * 128), f32),
            pltpu.VMEM((4, 32, KEPT * 128), f32),
            pltpu.VMEM((4, 2, 4, 32, KEPT * 128), f32),
            pltpu.VMEM((4, 2, 2, 2, 32, KEPT * 128), f32),
            pltpu.VMEM((1024, 1024), bf16),
            pltpu.VMEM((1024, 1024), bf16),
            pltpu.VMEM((1024, 1024), bf16),
            pltpu.VMEM((1024, 1024), bf16),
            pltpu.VMEM((1024, WIDE), bf16),
            pltpu.VMEM((1024, WIDE), bf16),
            pltpu.VMEM((1024, 1024), bf16),
            pltpu.VMEM((1024, 1024), bf16),
            pltpu.VMEM((8, 128, 1024), f32),
            dma((2, 8)), dma((2, KEPT)),
            dma((4, 2, PARTS)), dma((8, PARTS)),
            dma((2,)), dma((4,)), dma((3,)), dma((2,)), dma((2, 2)), dma((2, 2)), dma((2,)), dma((2,)),
            dma((4,)), dma((4,)), dma((2,)), dma((2,)), dma((4,)), dma((4,)), dma((2,)), dma((2,)),
            dma((4, 2)), dma((8,)),
        ],
        compiler_params=pltpu.CompilerParams(
            collective_id=0, has_side_effects=True, vmem_limit_bytes=56 * 2**20
        ),
        cost_estimate=pl.CostEstimate(flops=3 * 2**32, bytes_accessed=20 * 2**20, transcendentals=0),
    )(grad, momentum, left, right)


def per_device(grad, momentum, variance, weight, left_inverse, right_inverse):
    precond = precondition(grad, momentum, left_inverse, right_inverse)
    momentum_next = first_decay * momentum + (1.0 - first_decay) * grad.astype(jnp.float32)
    variance_next = second_decay * variance + (1.0 - second_decay) * precond * precond
    weight_float = weight.astype(jnp.float32)
    weight_next = weight_float - learn_rate * (
        precond / (jnp.sqrt(variance_next) + epsilon) + weight_decay * weight_float
    )
    return (momentum_next, variance_next, weight_next.astype(jnp.bfloat16))


def solution(mesh):
    torus = Mesh(mesh.devices.reshape(4, 2, 2, 2, 4), AXES)
    tiles = P(None, ("y", "a"), ("h", "k", "z"))
    in_specs = (
        tiles,
        tiles,
        tiles,
        tiles,
        P(("h", "k"), ("y", "a", "z"), None),
        P(None, "z", ("y", "a", "h", "k"), None),
    )
    return jax.shard_map(
        per_device, mesh=torus, in_specs=in_specs, out_specs=(tiles, tiles, tiles), check_vma=False
    )
```

```python
import functools

import jax
import jax.numpy as jnp
from jax import lax
from jax.experimental import pallas as pl
from jax.experimental.pallas import tpu as pltpu
from jax.sharding import Mesh
from jax.sharding import PartitionSpec as P

AXES = ("y", "a", "h", "k", "z")
MESH = pl.DeviceIdType.MESH

first_decay = 0.9
second_decay = 0.95
learn_rate = 0.1
weight_decay = 0.1
epsilon = 1e-08

PARTS = 4
WIDE = 1024 // PARTS
HOME_PARTS = 2
HOME_WIDE = 1024 // HOME_PARTS
KEPT = 5


def split(x):
    high = x.astype(jnp.bfloat16)
    low = (x - high.astype(jnp.float32)).astype(jnp.bfloat16)
    return high, low


def product(left_high, left_low, right_high, right_low):
    dot = functools.partial(jnp.dot, preferred_element_type=jnp.float32)
    return dot(left_high, right_high) + (dot(left_high, right_low) + dot(left_low, right_high))


def kernel(
    grad, momentum, variance, weight, left, right, own, variance_out, weight_out,
    grad_in, home_tile, tile, left_own, right_own, left_all, right_all, left_hi, left_lo, right_hi, right_lo,
    tile_hi, tile_lo, mixed_hi, mixed_lo, done,
    in_sem, pack_sem, late_sem, own_send, own_recv, l1_send, l1_recv, l2_send, l2_recv, l3_send, l3_recv, l4_send, l4_recv,
    r1_send, r1_recv, r2_send, r2_recv, r3_send, r3_recv, r4_send, r4_recv, p_send, p_recv,
):
    y, a, h, k, z = (lax.axis_index(name) for name in AXES)
    me_f = 2 * y + a

    def step(at, by):
        return lax.rem(at + by + 4, 4)

    def remote(src, dst, send, recv, device):
        return pltpu.make_async_remote_copy(
            src_ref=src, dst_ref=dst, send_sem=send, recv_sem=recv, device_id=device, device_id_type=MESH
        )

    def arrived(dst, recv):
        pltpu.make_async_copy(dst, dst, recv).wait()

    packs = []
    for d in range(KEPT):
        columns = pl.ds(pl.multiple_of(lax.rem(me_f + d, 8) * 128, 128), 128)
        packed = pl.ds(d * 128, 128)
        packs.append(pltpu.make_async_copy(left.at[:, :, columns], left_own.at[:, :, packed], pack_sem.at[0, d]))
        packs.append(pltpu.make_async_copy(right.at[:, 0, :, columns], right_own.at[:, :, packed], pack_sem.at[1, d]))
    for copy in packs:
        copy.start()
    loads = []
    for b in range(8):
        pair = (
            pltpu.make_async_copy(momentum.at[b], own.at[b], in_sem.at[0, b]),
            pltpu.make_async_copy(grad.at[b], grad_in.at[b], in_sem.at[1, b]),
        )
        for copy in pair:
            copy.start()
        loads.append(pair)
    late = [
        pltpu.make_async_copy(variance, variance_out, late_sem.at[0]),
        pltpu.make_async_copy(weight, weight_out, late_sem.at[1]),
    ]

    for copy in late:
        copy.start()

    barrier = pltpu.get_barrier_semaphore()
    others = []
    for dy in range(4):
        for da in range(2):
            for dk in range(2):
                if (dy, da, dk) != (0, 0, 0):
                    others.append((step(y, dy), lax.rem(a + da, 2), h, lax.rem(k + dk, 2), z))
    for da in range(2):
        others.append((y, lax.rem(a + da, 2), 1 - h, k, z))
    for dz in range(1, 4):
        others.append((y, a, h, k, step(z, dz)))
    for device in others:
        pl.semaphore_signal(barrier, inc=1, device_id=device, device_id_type=MESH)
    for b in range(8):
        for copy in loads[b]:
            copy.wait()

        @pl.loop(0, 4)
        def _(i):
            rows = pl.ds(pl.multiple_of(i * 32, 32), 32)
            own[b, rows] = first_decay * own[b, rows] + (1.0 - first_decay) * grad_in[b, rows].astype(jnp.float32)

    for copy in packs + late:
        copy.wait()
    pl.semaphore_wait(barrier, len(others))

    home = 2 * h + k
    holder = h == y // 2

    def l1(t):
        return remote(
            left_own.at[t], left_all.at[y, a, z], l1_send.at[t], l1_recv.at[y], (home, a, h, jnp.int32(t), z)
        )

    for t in range(2):
        stays = jnp.logical_and(y == home, k == t)

        @pl.when(stays)
        def _():
            pltpu.make_async_copy(left_own.at[t], left_all.at[y, a, z], l1_recv.at[y]).start()

        @pl.when(jnp.logical_not(stays))
        def _():
            l1(t).start()

    def r1(i):
        to_a, to_h = lax.rem(a + i % 2, 2), lax.rem(h + i // 2, 2)
        return remote(
            right_own.at[2 * to_h + to_a], right_all.at[y, a, h, k], r1_send.at[i], r1_recv.at[i], (y, to_a, to_h, k, z)
        )

    pltpu.make_async_copy(right_own.at[2 * h + a], right_all.at[y, a, h, k], r1_recv.at[0]).start()
    for i in range(1, 4):
        r1(i).start()

    def own_part(dy, t, part):
        to_y = step(y, dy)
        columns = pl.ds(part * WIDE, WIDE)
        return (
            own.at[2 * to_y + t, :, columns],
            tile.at[me_f, :, columns],
            own_send.at[dy, t, part],
            own_recv.at[me_f, part],
            (to_y, k, h, jnp.int32(t), z),
        )

    def send_part(part):
        for dy in (2, 1, 3, 0):
            for t in range(2):
                src, dst, send, recv, device = own_part(dy, t, part)
                if dy == 0:
                    stays = jnp.logical_and(a == k, k == t)

                    @pl.when(stays)
                    def _():
                        pltpu.make_async_copy(src, dst, recv).start()

                    @pl.when(jnp.logical_not(stays))
                    def _():
                        remote(src, dst, send, recv, device).start()
                else:
                    remote(src, dst, send, recv, device).start()

    send_part(0)

    def l2(i, from_y):
        rows = left_all.at[from_y, a, z]
        device = (y, lax.rem(a + i % 2, 2), lax.rem(h + i // 2, 2), k, z)
        return remote(rows, rows, l2_send.at[i - 1, from_y], l2_recv.at[a, from_y], device)

    def l3(from_a, s, from_y):
        rows = left_all.at[from_y, from_a, z]
        return remote(
            rows, rows, l3_send.at[from_a, s, from_y], l3_recv.at[from_a, s, from_y], (y, a, h, k, step(z, 1 - 2 * s))
        )

    def l4(s, from_y):
        rows = left_all.at[from_y, s, step(z, 2 * s - 1)]
        return remote(rows, rows, l4_send.at[s, from_y], l4_recv.at[s, from_y], (y, a, h, k, step(z, 1 - 2 * s)))

    @pl.when(holder)
    def _():
        for dy in (0, 1, 3, 2):
            from_y = step(y, dy)
            arrived(left_all.at[from_y, a, z], l1_recv.at[from_y])
            for i in (2, 3, 1):
                l2(i, from_y).start()
            for s in range(2):
                l3(a, s, from_y).start()

    def r2(s):
        rows = right_all.at[y, :, :, k]
        return remote(rows, rows, r2_send.at[s], r2_recv.at[s], (step(y, 1 - 2 * s), a, h, k, z))

    def r3(dy):
        rows = right_all.at[step(y, -dy), :, :, k]
        return remote(rows, rows, r3_send.at[dy], r3_recv.at[dy], (y, a, h, 1 - k, z))

    def r4(s):
        rows = right_all.at[step(y, 2 * s - 1), s, :, k]
        return remote(rows, rows, r4_send.at[s], r4_recv.at[s], (step(y, 1 - 2 * s), a, h, k, z))

    for i in range(4):
        arrived(right_all.at[y, lax.rem(a + i % 2, 2), lax.rem(h + i // 2, 2), k], r1_recv.at[i])
    for s in range(2):
        r2(s).start()
    r3(0).start()
    send_part(1)
    for dy in (0, 1, 3, 2):
        from_y = step(y, dy)

        @pl.when(jnp.logical_not(holder))
        def _():
            arrived(left_all.at[from_y, a, z], l2_recv.at[a, from_y])
            for s in range(2):
                l3(a, s, from_y).start()

        arrived(left_all.at[from_y, 1 - a, z], l2_recv.at[1 - a, from_y])
        for s in range(2):
            l3(1 - a, s, from_y).start()
    for part in range(2, PARTS):
        send_part(part)

    for s in range(2):
        arrived(right_all.at[step(y, 2 * s - 1), :, :, k], r2_recv.at[s])
        r4(s).start()
        r3(1 + 2 * s).start()
    for dy in (0, 1, 3, 2):
        for s in range(2):
            from_y = step(y, dy)
            arrived(left_all.at[from_y, s, step(z, 2 * s - 1)], l3_recv.at[s, s, from_y])
            l4(s, from_y).start()
    for s in range(2):
        arrived(right_all.at[step(y, 2), s, :, k], r4_recv.at[s])
    r3(2).start()
    for s in range(2):
        for from_y in range(4):
            arrived(left_all.at[from_y, 1 - s, step(z, 2 * s - 1)], l3_recv.at[1 - s, s, from_y])
            arrived(left_all.at[from_y, s, step(z, 2)], l4_recv.at[s, from_y])

    def unpack(rows_of, high, low):
        @pl.loop(0, 8)
        def _(f):
            at = pl.ds(pl.multiple_of(f * 128, 128), 128)
            for d in range(KEPT):
                block = rows_of(f, pl.ds(d * 128, 128)).reshape(128, 128)
                to = pl.ds(pl.multiple_of(lax.rem(f + d, 8) * 128, 128), 128)
                high[at, to], low[at, to] = split(block)
                if 0 < d < 4:
                    high[to, at], low[to, at] = split(block.T)

    unpack(lambda f, c: left_all[f // 2, lax.rem(f, 2), :, :, c], left_hi, left_lo)

    def left_rows(rows, columns):
        mixed = product(left_hi[rows], left_lo[rows], tile_hi[...], tile_lo[...])
        mixed_hi[rows, columns], mixed_lo[rows, columns] = split(mixed)

    for part in range(PARTS):
        columns = slice(part * WIDE, (part + 1) * WIDE)
        if part == PARTS - 1:
            for dy in (0, 1, 3, 2):
                arrived(right_all.at[step(y, -dy), :, :, 1 - k], r3_recv.at[dy])
            unpack(lambda f, c: right_all[f // 2, lax.rem(f, 2), :, :, :, c], right_hi, right_lo)
        for f in range(8):
            arrived(tile.at[f, :, columns], own_recv.at[f, part])

        @pl.loop(0, 8)
        def _(f):
            rows = pl.ds(pl.multiple_of(f * 128, 128), 128)
            tile_hi[rows], tile_lo[rows] = split(tile[f, :, columns])

        if part < PARTS - 1:

            @pl.loop(0, 4)
            def _(i):
                left_rows(pl.ds(pl.multiple_of(i * 256, 256), 256), columns)

    def p_copy(dy, to_a, part):
        to_y = step(y, dy)
        columns = pl.ds(part * HOME_WIDE, HOME_WIDE)
        return (
            done.at[2 * to_y + to_a, :, columns],
            home_tile.at[2 * y + k, :, columns],
            p_send.at[dy, to_a, part],
            p_recv.at[2 * y + k, part],
            (to_y, jnp.int32(to_a), h, a, z),
        )

    for dy in (2, 1, 3, 0):
        to_y = step(y, dy)
        rows = pl.ds(pl.multiple_of(to_y * 256, 256), 256)
        left_rows(rows, columns)
        for part in range(HOME_PARTS):

            @pl.loop(0, HOME_WIDE // 256)
            def _(i):
                here = pl.ds(pl.multiple_of(part * HOME_WIDE + i * 256, 256), 256)
                both = product(mixed_hi[rows], mixed_lo[rows], right_hi[:, here], right_lo[:, here])
                done[2 * to_y, :, here] = both[:128]
                done[2 * to_y + 1, :, here] = both[128:]

            for to_a in range(2):
                src, dst, send, recv, device = p_copy(dy, to_a, part)
                if dy == 0:
                    stays = jnp.logical_and(a == k, a == to_a)

                    @pl.when(stays)
                    def _():
                        pltpu.make_async_copy(src, dst, recv).start()

                    @pl.when(jnp.logical_not(stays))
                    def _():
                        remote(src, dst, send, recv, device).start()
                else:
                    remote(src, dst, send, recv, device).start()

    for dy in (2, 1, 3, 0):
        for t in range(2):
            b = 2 * step(y, -dy) + t
            for part in range(HOME_PARTS):
                columns = pl.ds(part * HOME_WIDE, HOME_WIDE)
                arrived(home_tile.at[b, :, columns], p_recv.at[b, part])

            @pl.loop(0, 8)
            def _(i):
                rows = pl.ds(pl.multiple_of(i * 16, 16), 16)
                precond = home_tile[b, rows]
                variance_next = second_decay * variance_out[b, rows] + (1.0 - second_decay) * precond * precond
                weight_float = weight_out[b, rows].astype(jnp.float32)
                weight_next = weight_float - learn_rate * (
                    precond / (jnp.sqrt(variance_next) + epsilon) + weight_decay * weight_float
                )
                variance_out[b, rows] = variance_next
                weight_out[b, rows] = weight_next.astype(jnp.bfloat16)

    for t in range(2):

        @pl.when(jnp.logical_not(jnp.logical_and(y == home, k == t)))
        def _():
            l1(t).wait_send()

    for i in range(1, 4):
        r1(i).wait_send()

    @pl.when(holder)
    def _():
        for i in range(1, 4):
            for from_y in range(4):
                l2(i, from_y).wait_send()

    for s in range(2):
        for from_y in range(4):
            l3(0, s, from_y).wait_send()
            l3(1, s, from_y).wait_send()
            l4(s, from_y).wait_send()
        r2(s).wait_send()
        r4(s).wait_send()
    for dy in range(4):
        r3(dy).wait_send()
    for dy in range(4):
        for t in range(2):
            sends = [remote(*own_part(dy, t, part)) for part in range(PARTS)]
            sends += [remote(*p_copy(dy, t, part)) for part in range(HOME_PARTS)]
            if dy == 0:

                @pl.when(jnp.logical_not(jnp.logical_and(a == k, k == t)))
                def _():
                    for copy in sends:
                        copy.wait_send()
            else:
                for copy in sends:
                    copy.wait_send()
def store(momentum, variance, weight, momentum_out, variance_out, weight_out, sem):
    copies = [
        pltpu.make_async_copy(src.at[pl.ds(2 * i, 2)], dst.at[pl.ds(2 * i, 2)], sem.at[n, i])
        for i in range(4)
        for n, (src, dst) in enumerate(((momentum, momentum_out), (variance, variance_out), (weight, weight_out)))
    ]
    for copy in copies:
        copy.start()
    for copy in copies:
        copy.wait()


def update(grad, momentum, variance, weight, left, right):
    f32, bf16 = jnp.float32, jnp.bfloat16
    dma = pltpu.SemaphoreType.DMA
    updated = pl.pallas_call(
        kernel,
        out_shape=(
            pltpu.VMEM((8, 128, 1024), f32),
            pltpu.VMEM((8, 128, 1024), f32),
            pltpu.VMEM((8, 128, 1024), bf16),
        ),
        in_specs=[pl.BlockSpec(memory_space=pl.ANY)] * 6,
        out_specs=(pl.BlockSpec(memory_space=pltpu.VMEM),) * 3,
        scratch_shapes=[
            pltpu.VMEM((8, 128, 1024), bf16),
            pltpu.VMEM((8, 128, 1024), f32),
            pltpu.VMEM((8, 128, 1024), f32),
            pltpu.VMEM((2, 32, KEPT * 128), f32),
            pltpu.VMEM((4, 32, KEPT * 128), f32),
            pltpu.VMEM((4, 2, 4, 32, KEPT * 128), f32),
            pltpu.VMEM((4, 2, 2, 2, 32, KEPT * 128), f32),
            pltpu.VMEM((1024, 1024), bf16),
            pltpu.VMEM((1024, 1024), bf16),
            pltpu.VMEM((1024, 1024), bf16),
            pltpu.VMEM((1024, 1024), bf16),
            pltpu.VMEM((1024, WIDE), bf16),
            pltpu.VMEM((1024, WIDE), bf16),
            pltpu.VMEM((1024, 1024), bf16),
            pltpu.VMEM((1024, 1024), bf16),
            pltpu.VMEM((8, 128, 1024), f32),
            dma((2, 8)), dma((2, KEPT)), dma((2,)),
            dma((4, 2, PARTS)), dma((8, PARTS)),
            dma((2,)), dma((4,)), dma((3, 4)), dma((2, 4)), dma((2, 2, 4)), dma((2, 2, 4)), dma((2, 4)), dma((2, 4)),
            dma((4,)), dma((4,)), dma((2,)), dma((2,)), dma((4,)), dma((4,)), dma((2,)), dma((2,)),
            dma((4, 2, HOME_PARTS)), dma((8, HOME_PARTS)),
        ],
        compiler_params=pltpu.CompilerParams(
            collective_id=0, has_side_effects=True, vmem_limit_bytes=48 * 2**20
        ),
        cost_estimate=pl.CostEstimate(flops=3 * 2**32, bytes_accessed=20 * 2**20, transcendentals=0),
    )(grad, momentum, variance, weight, left, right)
    return pl.pallas_call(
        store,
        out_shape=[jax.ShapeDtypeStruct(x.shape, x.dtype) for x in updated],
        in_specs=[pl.BlockSpec(memory_space=pl.ANY)] * 3,
        out_specs=[pl.BlockSpec(memory_space=pl.ANY)] * 3,
        scratch_shapes=[dma((3, 4))],
        compiler_params=pltpu.CompilerParams(vmem_limit_bytes=2**20),
    )(*updated)


def solution(mesh):
    torus = Mesh(mesh.devices.reshape(4, 2, 2, 2, 4), AXES)
    tiles = P(None, ("y", "a"), ("h", "k", "z"))
    in_specs = (
        tiles,
        tiles,
        tiles,
        tiles,
        P(("h", "k"), ("y", "a", "z"), None),
        P(None, "z", ("y", "a", "h", "k"), None),
    )
    return jax.shard_map(
        update, mesh=torus, in_specs=in_specs, out_specs=(tiles, tiles, tiles), check_vma=False
    )
```

```python
import functools

import jax
import jax.numpy as jnp
from jax import lax
from jax.experimental import pallas as pl
from jax.experimental.pallas import tpu as pltpu
from jax.sharding import Mesh
from jax.sharding import PartitionSpec as P

AXES = ("y", "a", "h", "k", "z")
MESH = pl.DeviceIdType.MESH

first_decay = 0.9
second_decay = 0.95
learn_rate = 0.1
weight_decay = 0.1
epsilon = 1e-08

PARTS = 4
WIDE = 1024 // PARTS
HOME_PARTS = 2
HOME_WIDE = 1024 // HOME_PARTS
KEPT = 5


def split(x):
    high = x.astype(jnp.bfloat16)
    low = (x - high.astype(jnp.float32)).astype(jnp.bfloat16)
    return high, low


def product(left_high, left_low, right_high, right_low):
    dot = functools.partial(jnp.dot, preferred_element_type=jnp.float32)
    return dot(left_high, right_high) + (dot(left_high, right_low) + dot(left_low, right_high))


def kernel(
    grad, momentum, variance, weight, left, right, own, variance_out, weight_out,
    grad_in, home_tile, tile, left_own, right_own, left_all, right_all, left_hi, left_lo, right_hi, right_lo,
    tile_hi, tile_lo, mixed_hi, mixed_lo, done,
    in_sem, pack_sem, late_sem, own_send, own_recv, l1_send, l1_recv, l2_send, l2_recv, l3_send, l3_recv, l4_send, l4_recv,
    r1_send, r1_recv, r2_send, r2_recv, r3_send, r3_recv, r4_send, r4_recv, p_send, p_recv,
):
    y, a, h, k, z = (lax.axis_index(name) for name in AXES)
    me_f = 2 * y + a

    def step(at, by):
        return lax.rem(at + by + 4, 4)

    def remote(src, dst, send, recv, device):
        return pltpu.make_async_remote_copy(
            src_ref=src, dst_ref=dst, send_sem=send, recv_sem=recv, device_id=device, device_id_type=MESH
        )

    def arrived(dst, recv):
        pltpu.make_async_copy(dst, dst, recv).wait()

    packs = []
    for d in range(KEPT):
        columns = pl.ds(pl.multiple_of(lax.rem(me_f + d, 8) * 128, 128), 128)
        packed = pl.ds(d * 128, 128)
        packs.append(pltpu.make_async_copy(left.at[:, :, columns], left_own.at[:, :, packed], pack_sem.at[0, d]))
        packs.append(pltpu.make_async_copy(right.at[:, 0, :, columns], right_own.at[:, :, packed], pack_sem.at[1, d]))
    for copy in packs:
        copy.start()
    order = [(dy, t) for dy in (2, 1, 3, 0) for t in range(2)]
    loads = {}
    for dy, t in order:
        b = 2 * step(y, dy) + t
        loads[dy, t] = (
            pltpu.make_async_copy(momentum.at[b], own.at[b], in_sem.at[0, b]),
            pltpu.make_async_copy(grad.at[b], grad_in.at[b], in_sem.at[1, b]),
        )
        for copy in loads[dy, t]:
            copy.start()
    late = [
        pltpu.make_async_copy(variance, variance_out, late_sem.at[0]),
        pltpu.make_async_copy(weight, weight_out, late_sem.at[1]),
    ]

    for copy in late:
        copy.start()

    barrier = pltpu.get_barrier_semaphore()
    others = []
    for dy in range(4):
        for da in range(2):
            for dk in range(2):
                if (dy, da, dk) != (0, 0, 0):
                    others.append((step(y, dy), lax.rem(a + da, 2), h, lax.rem(k + dk, 2), z))
    for da in range(2):
        others.append((y, lax.rem(a + da, 2), 1 - h, k, z))
    for dz in range(1, 4):
        others.append((y, a, h, k, step(z, dz)))
    for device in others:
        pl.semaphore_signal(barrier, inc=1, device_id=device, device_id_type=MESH)
    for copy in packs:
        copy.wait()
    pl.semaphore_wait(barrier, len(others))

    home = 2 * h + k
    holder = h == y // 2

    def l1(t):
        return remote(
            left_own.at[t], left_all.at[y, a, z], l1_send.at[t], l1_recv.at[y], (home, a, h, jnp.int32(t), z)
        )

    for t in range(2):
        stays = jnp.logical_and(y == home, k == t)

        @pl.when(stays)
        def _():
            pltpu.make_async_copy(left_own.at[t], left_all.at[y, a, z], l1_recv.at[y]).start()

        @pl.when(jnp.logical_not(stays))
        def _():
            l1(t).start()

    def r1(i):
        to_a, to_h = lax.rem(a + i % 2, 2), lax.rem(h + i // 2, 2)
        return remote(
            right_own.at[2 * to_h + to_a], right_all.at[y, a, h, k], r1_send.at[i], r1_recv.at[i], (y, to_a, to_h, k, z)
        )

    pltpu.make_async_copy(right_own.at[2 * h + a], right_all.at[y, a, h, k], r1_recv.at[0]).start()
    for i in range(1, 4):
        r1(i).start()

    def own_part(dy, t, part):
        to_y = step(y, dy)
        columns = pl.ds(part * WIDE, WIDE)
        return (
            own.at[2 * to_y + t, :, columns],
            tile.at[me_f, :, columns],
            own_send.at[dy, t, part],
            own_recv.at[me_f, part],
            (to_y, k, h, jnp.int32(t), z),
        )

    def send_part(part, dy, t):
        src, dst, send, recv, device = own_part(dy, t, part)
        if dy == 0:
            stays = jnp.logical_and(a == k, k == t)

            @pl.when(stays)
            def _():
                pltpu.make_async_copy(src, dst, recv).start()

            @pl.when(jnp.logical_not(stays))
            def _():
                remote(src, dst, send, recv, device).start()
        else:
            remote(src, dst, send, recv, device).start()

    for dy, t in order:
        b = 2 * step(y, dy) + t
        for copy in loads[dy, t]:
            copy.wait()

        @pl.loop(0, 4)
        def _(i):
            rows = pl.ds(pl.multiple_of(i * 32, 32), 32)
            own[b, rows] = first_decay * own[b, rows] + (1.0 - first_decay) * grad_in[b, rows].astype(jnp.float32)

        send_part(0, dy, t)

    def l2(i, from_y):
        rows = left_all.at[from_y, a, z]
        device = (y, lax.rem(a + i % 2, 2), lax.rem(h + i // 2, 2), k, z)
        return remote(rows, rows, l2_send.at[i - 1, from_y], l2_recv.at[a, from_y], device)

    def l3(from_a, s, from_y):
        rows = left_all.at[from_y, from_a, z]
        return remote(
            rows, rows, l3_send.at[from_a, s, from_y], l3_recv.at[from_a, s, from_y], (y, a, h, k, step(z, 1 - 2 * s))
        )

    def l4(s, from_y):
        rows = left_all.at[from_y, s, step(z, 2 * s - 1)]
        return remote(rows, rows, l4_send.at[s, from_y], l4_recv.at[s, from_y], (y, a, h, k, step(z, 1 - 2 * s)))

    def r2(s):
        rows = right_all.at[y, :, :, k]
        return remote(rows, rows, r2_send.at[s], r2_recv.at[s], (step(y, 1 - 2 * s), a, h, k, z))

    def r3(dy):
        rows = right_all.at[step(y, -dy), :, :, k]
        return remote(rows, rows, r3_send.at[dy], r3_recv.at[dy], (y, a, h, 1 - k, z))

    def r4(s):
        rows = right_all.at[step(y, 2 * s - 1), s, :, k]
        return remote(rows, rows, r4_send.at[s], r4_recv.at[s], (step(y, 1 - 2 * s), a, h, k, z))

    @pl.when(holder)
    def _():
        for dy in (0, 1, 3, 2):
            from_y = step(y, dy)
            arrived(left_all.at[from_y, a, z], l1_recv.at[from_y])
            for i in (2, 3, 1):
                l2(i, from_y).start()
            for s in range(2):
                l3(a, s, from_y).start()

    for i in range(4):
        arrived(right_all.at[y, lax.rem(a + i % 2, 2), lax.rem(h + i // 2, 2), k], r1_recv.at[i])
    for s in range(2):
        r2(s).start()
    r3(0).start()
    for part in range(1, PARTS):
        for dy, t in order:
            send_part(part, dy, t)
    for dy in (0, 1, 3, 2):
        from_y = step(y, dy)

        @pl.when(jnp.logical_not(holder))
        def _():
            arrived(left_all.at[from_y, a, z], l2_recv.at[a, from_y])
            for s in range(2):
                l3(a, s, from_y).start()

        arrived(left_all.at[from_y, 1 - a, z], l2_recv.at[1 - a, from_y])
        for s in range(2):
            l3(1 - a, s, from_y).start()
    for s in range(2):
        arrived(right_all.at[step(y, 2 * s - 1), :, :, k], r2_recv.at[s])
        r4(s).start()
        r3(1 + 2 * s).start()
    for dy in (0, 1, 3, 2):
        for s in range(2):
            from_y = step(y, dy)
            arrived(left_all.at[from_y, s, step(z, 2 * s - 1)], l3_recv.at[s, s, from_y])
            l4(s, from_y).start()
    for s in range(2):
        arrived(right_all.at[step(y, 2), s, :, k], r4_recv.at[s])
    r3(2).start()
    for s in range(2):
        for from_y in range(4):
            arrived(left_all.at[from_y, 1 - s, step(z, 2 * s - 1)], l3_recv.at[1 - s, s, from_y])
            arrived(left_all.at[from_y, s, step(z, 2)], l4_recv.at[s, from_y])

    def unpack(rows_of, high, low):
        @pl.loop(0, 8)
        def _(f):
            at = pl.ds(pl.multiple_of(f * 128, 128), 128)
            for d in range(KEPT):
                block = rows_of(f, pl.ds(d * 128, 128)).reshape(128, 128)
                to = pl.ds(pl.multiple_of(lax.rem(f + d, 8) * 128, 128), 128)
                high[at, to], low[at, to] = split(block)
                if 0 < d < 4:
                    high[to, at], low[to, at] = split(block.T)

    unpack(lambda f, c: left_all[f // 2, lax.rem(f, 2), :, :, c], left_hi, left_lo)

    def left_rows(rows, columns):
        mixed = product(left_hi[rows], left_lo[rows], tile_hi[...], tile_lo[...])
        mixed_hi[rows, columns], mixed_lo[rows, columns] = split(mixed)

    for part in range(PARTS):
        columns = slice(part * WIDE, (part + 1) * WIDE)
        if part == PARTS - 1:
            for dy in (0, 1, 3, 2):
                arrived(right_all.at[step(y, -dy), :, :, 1 - k], r3_recv.at[dy])
            unpack(lambda f, c: right_all[f // 2, lax.rem(f, 2), :, :, :, c], right_hi, right_lo)
        for f in range(8):
            arrived(tile.at[f, :, columns], own_recv.at[f, part])

        @pl.loop(0, 8)
        def _(f):
            rows = pl.ds(pl.multiple_of(f * 128, 128), 128)
            tile_hi[rows], tile_lo[rows] = split(tile[f, :, columns])

        if part < PARTS - 1:

            @pl.loop(0, 4)
            def _(i):
                left_rows(pl.ds(pl.multiple_of(i * 256, 256), 256), columns)

    def p_copy(dy, to_a, part):
        to_y = step(y, dy)
        columns = pl.ds(part * HOME_WIDE, HOME_WIDE)
        return (
            done.at[2 * to_y + to_a, :, columns],
            home_tile.at[2 * y + k, :, columns],
            p_send.at[dy, to_a, part],
            p_recv.at[2 * y + k, part],
            (to_y, jnp.int32(to_a), h, a, z),
        )

    for dy in (2, 1, 3, 0):
        to_y = step(y, dy)
        rows = pl.ds(pl.multiple_of(to_y * 256, 256), 256)
        left_rows(rows, columns)
        for part in range(HOME_PARTS):

            @pl.loop(0, HOME_WIDE // 256)
            def _(i):
                here = pl.ds(pl.multiple_of(part * HOME_WIDE + i * 256, 256), 256)
                both = product(mixed_hi[rows], mixed_lo[rows], right_hi[:, here], right_lo[:, here])
                done[2 * to_y, :, here] = both[:128]
                done[2 * to_y + 1, :, here] = both[128:]

            for to_a in range(2):
                src, dst, send, recv, device = p_copy(dy, to_a, part)
                if dy == 0:
                    stays = jnp.logical_and(a == k, a == to_a)

                    @pl.when(stays)
                    def _():
                        pltpu.make_async_copy(src, dst, recv).start()

                    @pl.when(jnp.logical_not(stays))
                    def _():
                        remote(src, dst, send, recv, device).start()
                else:
                    remote(src, dst, send, recv, device).start()

    for copy in late:
        copy.wait()
    for dy in (2, 1, 3, 0):
        for t in range(2):
            b = 2 * step(y, -dy) + t
            for part in range(HOME_PARTS):
                columns = pl.ds(part * HOME_WIDE, HOME_WIDE)
                arrived(home_tile.at[b, :, columns], p_recv.at[b, part])

            @pl.loop(0, 8)
            def _(i):
                rows = pl.ds(pl.multiple_of(i * 16, 16), 16)
                precond = home_tile[b, rows]
                variance_next = second_decay * variance_out[b, rows] + (1.0 - second_decay) * precond * precond
                weight_float = weight_out[b, rows].astype(jnp.float32)
                weight_next = weight_float - learn_rate * (
                    precond / (jnp.sqrt(variance_next) + epsilon) + weight_decay * weight_float
                )
                variance_out[b, rows] = variance_next
                weight_out[b, rows] = weight_next.astype(jnp.bfloat16)

    for t in range(2):

        @pl.when(jnp.logical_not(jnp.logical_and(y == home, k == t)))
        def _():
            l1(t).wait_send()

    for i in range(1, 4):
        r1(i).wait_send()

    @pl.when(holder)
    def _():
        for i in range(1, 4):
            for from_y in range(4):
                l2(i, from_y).wait_send()

    for s in range(2):
        for from_y in range(4):
            l3(0, s, from_y).wait_send()
            l3(1, s, from_y).wait_send()
            l4(s, from_y).wait_send()
        r2(s).wait_send()
        r4(s).wait_send()
    for dy in range(4):
        r3(dy).wait_send()
    for dy in range(4):
        for t in range(2):
            sends = [remote(*own_part(dy, t, part)) for part in range(PARTS)]
            sends += [remote(*p_copy(dy, t, part)) for part in range(HOME_PARTS)]
            if dy == 0:

                @pl.when(jnp.logical_not(jnp.logical_and(a == k, k == t)))
                def _():
                    for copy in sends:
                        copy.wait_send()
            else:
                for copy in sends:
                    copy.wait_send()
def store(momentum, variance, weight, momentum_out, variance_out, weight_out, sem):
    copies = [
        pltpu.make_async_copy(src.at[pl.ds(2 * i, 2)], dst.at[pl.ds(2 * i, 2)], sem.at[n, i])
        for i in range(4)
        for n, (src, dst) in enumerate(((momentum, momentum_out), (variance, variance_out), (weight, weight_out)))
    ]
    for copy in copies:
        copy.start()
    for copy in copies:
        copy.wait()


def update(grad, momentum, variance, weight, left, right):
    f32, bf16 = jnp.float32, jnp.bfloat16
    dma = pltpu.SemaphoreType.DMA
    updated = pl.pallas_call(
        kernel,
        out_shape=(
            pltpu.VMEM((8, 128, 1024), f32),
            pltpu.VMEM((8, 128, 1024), f32),
            pltpu.VMEM((8, 128, 1024), bf16),
        ),
        in_specs=[pl.BlockSpec(memory_space=pl.ANY)] * 6,
        out_specs=(pl.BlockSpec(memory_space=pltpu.VMEM),) * 3,
        scratch_shapes=[
            pltpu.VMEM((8, 128, 1024), bf16),
            pltpu.VMEM((8, 128, 1024), f32),
            pltpu.VMEM((8, 128, 1024), f32),
            pltpu.VMEM((2, 32, KEPT * 128), f32),
            pltpu.VMEM((4, 32, KEPT * 128), f32),
            pltpu.VMEM((4, 2, 4, 32, KEPT * 128), f32),
            pltpu.VMEM((4, 2, 2, 2, 32, KEPT * 128), f32),
            pltpu.VMEM((1024, 1024), bf16),
            pltpu.VMEM((1024, 1024), bf16),
            pltpu.VMEM((1024, 1024), bf16),
            pltpu.VMEM((1024, 1024), bf16),
            pltpu.VMEM((1024, WIDE), bf16),
            pltpu.VMEM((1024, WIDE), bf16),
            pltpu.VMEM((1024, 1024), bf16),
            pltpu.VMEM((1024, 1024), bf16),
            pltpu.VMEM((8, 128, 1024), f32),
            dma((2, 8)), dma((2, KEPT)), dma((2,)),
            dma((4, 2, PARTS)), dma((8, PARTS)),
            dma((2,)), dma((4,)), dma((3, 4)), dma((2, 4)), dma((2, 2, 4)), dma((2, 2, 4)), dma((2, 4)), dma((2, 4)),
            dma((4,)), dma((4,)), dma((2,)), dma((2,)), dma((4,)), dma((4,)), dma((2,)), dma((2,)),
            dma((4, 2, HOME_PARTS)), dma((8, HOME_PARTS)),
        ],
        compiler_params=pltpu.CompilerParams(
            collective_id=0, has_side_effects=True, vmem_limit_bytes=48 * 2**20
        ),
        cost_estimate=pl.CostEstimate(flops=3 * 2**32, bytes_accessed=20 * 2**20, transcendentals=0),
    )(grad, momentum, variance, weight, left, right)
    return pl.pallas_call(
        store,
        out_shape=[jax.ShapeDtypeStruct(x.shape, x.dtype) for x in updated],
        in_specs=[pl.BlockSpec(memory_space=pl.ANY)] * 3,
        out_specs=[pl.BlockSpec(memory_space=pl.ANY)] * 3,
        scratch_shapes=[dma((3, 4))],
        compiler_params=pltpu.CompilerParams(vmem_limit_bytes=2**20),
    )(*updated)


def solution(mesh):
    torus = Mesh(mesh.devices.reshape(4, 2, 2, 2, 4), AXES)
    tiles = P(None, ("y", "a"), ("h", "k", "z"))
    in_specs = (
        tiles,
        tiles,
        tiles,
        tiles,
        P(("h", "k"), ("y", "a", "z"), None),
        P(None, "z", ("y", "a", "h", "k"), None),
    )
    return jax.shard_map(
        update, mesh=torus, in_specs=in_specs, out_specs=(tiles, tiles, tiles), check_vma=False
    )
```

```python
import functools

import jax
import jax.numpy as jnp
from jax import lax
from jax.experimental import pallas as pl
from jax.experimental.pallas import tpu as pltpu
from jax.sharding import Mesh
from jax.sharding import PartitionSpec as P

AXES = ("y", "a", "h", "k", "z")
MESH = pl.DeviceIdType.MESH

first_decay = 0.9
second_decay = 0.95
learn_rate = 0.1
weight_decay = 0.1
epsilon = 1e-08

PARTS = 4
WIDE = 1024 // PARTS
HOME_PARTS = 2
HOME_WIDE = 1024 // HOME_PARTS
KEPT = 5


def split(x):
    high = x.astype(jnp.bfloat16)
    low = (x - high.astype(jnp.float32)).astype(jnp.bfloat16)
    return high, low


def product(left_high, left_low, right_high, right_low):
    dot = functools.partial(jnp.dot, preferred_element_type=jnp.float32)
    return dot(left_high, right_high) + (dot(left_high, right_low) + dot(left_low, right_high))


def kernel(
    grad, momentum, variance, weight, left, right, own, variance_out, weight_out,
    grad_in, home_tile, tile, left_own, right_own, left_all, right_all, left_hi, left_lo, right_hi, right_lo,
    tile_hi, tile_lo, mixed_hi, mixed_lo, done,
    in_sem, pack_sem, late_sem, own_send, own_recv, l1_send, l1_recv, l2_send, l2_recv, l3_send, l3_recv, l4_send, l4_recv,
    r1_send, r1_recv, r2_send, r2_recv, r3_send, r3_recv, r4_send, r4_recv, p_send, p_recv,
):
    y, a, h, k, z = (lax.axis_index(name) for name in AXES)
    me_f = 2 * y + a

    def step(at, by):
        return lax.rem(at + by + 4, 4)

    def plane(dy):
        return step(y, dy * (1 - 2 * k))

    def remote(src, dst, send, recv, device):
        return pltpu.make_async_remote_copy(
            src_ref=src, dst_ref=dst, send_sem=send, recv_sem=recv, device_id=device, device_id_type=MESH
        )

    def arrived(dst, recv):
        pltpu.make_async_copy(dst, dst, recv).wait()

    packs = []
    for d in range(KEPT):
        columns = pl.ds(pl.multiple_of(lax.rem(me_f + d, 8) * 128, 128), 128)
        packed = pl.ds(d * 128, 128)
        packs.append(pltpu.make_async_copy(left.at[:, :, columns], left_own.at[:, :, packed], pack_sem.at[0, d]))
        packs.append(pltpu.make_async_copy(right.at[:, 0, :, columns], right_own.at[:, :, packed], pack_sem.at[1, d]))
    for copy in packs:
        copy.start()
    order = [(dy, t) for dy in (2, 1, 3, 0) for t in range(2)]
    loads = {}
    for dy, t in order:
        b = 2 * plane(dy) + t
        loads[dy, t] = (
            pltpu.make_async_copy(momentum.at[b], own.at[b], in_sem.at[0, b]),
            pltpu.make_async_copy(grad.at[b], grad_in.at[b], in_sem.at[1, b]),
        )
        for copy in loads[dy, t]:
            copy.start()
    late = [
        pltpu.make_async_copy(variance, variance_out, late_sem.at[0]),
        pltpu.make_async_copy(weight, weight_out, late_sem.at[1]),
    ]

    for copy in late:
        copy.start()

    barrier = pltpu.get_barrier_semaphore()
    others = []
    for dy in range(4):
        for da in range(2):
            for dk in range(2):
                if (dy, da, dk) != (0, 0, 0):
                    others.append((step(y, dy), lax.rem(a + da, 2), h, lax.rem(k + dk, 2), z))
    for da in range(2):
        others.append((y, lax.rem(a + da, 2), 1 - h, k, z))
    for dz in range(1, 4):
        others.append((y, a, h, k, step(z, dz)))
    for device in others:
        pl.semaphore_signal(barrier, inc=1, device_id=device, device_id_type=MESH)
    for copy in packs:
        copy.wait()
    pl.semaphore_wait(barrier, len(others))

    home = 2 * h + k
    holder = h == y // 2

    def l1(t):
        return remote(
            left_own.at[t], left_all.at[y, a, z], l1_send.at[t], l1_recv.at[y], (home, a, h, jnp.int32(t), z)
        )

    for t in range(2):
        stays = jnp.logical_and(y == home, k == t)

        @pl.when(stays)
        def _():
            pltpu.make_async_copy(left_own.at[t], left_all.at[y, a, z], l1_recv.at[y]).start()

        @pl.when(jnp.logical_not(stays))
        def _():
            l1(t).start()

    def r1(i):
        to_a, to_h = lax.rem(a + i % 2, 2), lax.rem(h + i // 2, 2)
        return remote(
            right_own.at[2 * to_h + to_a], right_all.at[y, a, h, k], r1_send.at[i], r1_recv.at[i], (y, to_a, to_h, k, z)
        )

    pltpu.make_async_copy(right_own.at[2 * h + a], right_all.at[y, a, h, k], r1_recv.at[0]).start()
    for i in range(1, 4):
        r1(i).start()

    def own_part(dy, t, part):
        to_y = plane(dy)
        columns = pl.ds(part * WIDE, WIDE)
        return (
            own.at[2 * to_y + t, :, columns],
            tile.at[me_f, :, columns],
            own_send.at[dy, t, part],
            own_recv.at[me_f, part],
            (to_y, k, h, jnp.int32(t), z),
        )

    def send_part(part, dy, t):
        src, dst, send, recv, device = own_part(dy, t, part)
        if dy == 0:
            stays = jnp.logical_and(a == k, k == t)

            @pl.when(stays)
            def _():
                pltpu.make_async_copy(src, dst, recv).start()

            @pl.when(jnp.logical_not(stays))
            def _():
                remote(src, dst, send, recv, device).start()
        else:
            remote(src, dst, send, recv, device).start()

    for dy, t in order:
        b = 2 * plane(dy) + t
        for copy in loads[dy, t]:
            copy.wait()

        @pl.loop(0, 4)
        def _(i):
            rows = pl.ds(pl.multiple_of(i * 32, 32), 32)
            own[b, rows] = first_decay * own[b, rows] + (1.0 - first_decay) * grad_in[b, rows].astype(jnp.float32)

        send_part(0, dy, t)

    def l2(i, from_y):
        rows = left_all.at[from_y, a, z]
        device = (y, lax.rem(a + i % 2, 2), lax.rem(h + i // 2, 2), k, z)
        return remote(rows, rows, l2_send.at[i - 1, from_y], l2_recv.at[a, from_y], device)

    def l3(from_a, s, from_y):
        rows = left_all.at[from_y, from_a, z]
        return remote(
            rows, rows, l3_send.at[from_a, s, from_y], l3_recv.at[from_a, s, from_y], (y, a, h, k, step(z, 1 - 2 * s))
        )

    def l4(s, from_y):
        rows = left_all.at[from_y, s, step(z, 2 * s - 1)]
        return remote(rows, rows, l4_send.at[s, from_y], l4_recv.at[s, from_y], (y, a, h, k, step(z, 1 - 2 * s)))

    def r2(s):
        rows = right_all.at[y, :, :, k]
        return remote(rows, rows, r2_send.at[s], r2_recv.at[s], (step(y, 1 - 2 * s), a, h, k, z))

    def r3(dy):
        rows = right_all.at[step(y, -dy), :, :, k]
        return remote(rows, rows, r3_send.at[dy], r3_recv.at[dy], (y, a, h, 1 - k, z))

    def r4(s):
        rows = right_all.at[step(y, 2 * s - 1), s, :, k]
        return remote(rows, rows, r4_send.at[s], r4_recv.at[s], (step(y, 1 - 2 * s), a, h, k, z))

    @pl.when(holder)
    def _():
        for dy in (0, 1, 3, 2):
            from_y = step(y, dy)
            arrived(left_all.at[from_y, a, z], l1_recv.at[from_y])
            for i in (2, 3, 1):
                l2(i, from_y).start()
            for s in range(2):
                l3(a, s, from_y).start()

    for i in range(4):
        arrived(right_all.at[y, lax.rem(a + i % 2, 2), lax.rem(h + i // 2, 2), k], r1_recv.at[i])
    for s in range(2):
        r2(s).start()
    r3(0).start()
    for part in range(1, PARTS):
        for dy, t in order:
            send_part(part, dy, t)
    for dy in (0, 1, 3, 2):
        from_y = step(y, dy)

        @pl.when(jnp.logical_not(holder))
        def _():
            arrived(left_all.at[from_y, a, z], l2_recv.at[a, from_y])
            for s in range(2):
                l3(a, s, from_y).start()

        arrived(left_all.at[from_y, 1 - a, z], l2_recv.at[1 - a, from_y])
        for s in range(2):
            l3(1 - a, s, from_y).start()
    for s in range(2):
        arrived(right_all.at[step(y, 2 * s - 1), :, :, k], r2_recv.at[s])
        r4(s).start()
        r3(1 + 2 * s).start()
    for dy in (0, 1, 3, 2):
        for s in range(2):
            from_y = step(y, dy)
            arrived(left_all.at[from_y, s, step(z, 2 * s - 1)], l3_recv.at[s, s, from_y])
            l4(s, from_y).start()
    for s in range(2):
        arrived(right_all.at[step(y, 2), s, :, k], r4_recv.at[s])
    r3(2).start()
    for s in range(2):
        for from_y in range(4):
            arrived(left_all.at[from_y, 1 - s, step(z, 2 * s - 1)], l3_recv.at[1 - s, s, from_y])
            arrived(left_all.at[from_y, s, step(z, 2)], l4_recv.at[s, from_y])

    def unpack(rows_of, high, low):
        @pl.loop(0, 8)
        def _(f):
            at = pl.ds(pl.multiple_of(f * 128, 128), 128)
            for d in range(KEPT):
                block = rows_of(f, pl.ds(d * 128, 128)).reshape(128, 128)
                to = pl.ds(pl.multiple_of(lax.rem(f + d, 8) * 128, 128), 128)
                high[at, to], low[at, to] = split(block)
                if 0 < d < 4:
                    high[to, at], low[to, at] = split(block.T)

    unpack(lambda f, c: left_all[f // 2, lax.rem(f, 2), :, :, c], left_hi, left_lo)

    def left_rows(rows, columns):
        mixed = product(left_hi[rows], left_lo[rows], tile_hi[...], tile_lo[...])
        mixed_hi[rows, columns], mixed_lo[rows, columns] = split(mixed)

    for part in range(PARTS):
        columns = slice(part * WIDE, (part + 1) * WIDE)
        if part == PARTS - 1:
            for dy in (0, 1, 3, 2):
                arrived(right_all.at[step(y, -dy), :, :, 1 - k], r3_recv.at[dy])
            unpack(lambda f, c: right_all[f // 2, lax.rem(f, 2), :, :, :, c], right_hi, right_lo)
        for f in range(8):
            arrived(tile.at[f, :, columns], own_recv.at[f, part])

        @pl.loop(0, 8)
        def _(f):
            rows = pl.ds(pl.multiple_of(f * 128, 128), 128)
            tile_hi[rows], tile_lo[rows] = split(tile[f, :, columns])

        if part < PARTS - 1:

            @pl.loop(0, 4)
            def _(i):
                left_rows(pl.ds(pl.multiple_of(i * 256, 256), 256), columns)

    def p_copy(dy, to_a, part):
        to_y = plane(dy)
        columns = pl.ds(part * HOME_WIDE, HOME_WIDE)
        return (
            done.at[2 * to_y + to_a, :, columns],
            home_tile.at[2 * y + k, :, columns],
            p_send.at[dy, to_a, part],
            p_recv.at[2 * y + k, part],
            (to_y, jnp.int32(to_a), h, a, z),
        )

    for dy in (2, 1, 3, 0):
        to_y = plane(dy)
        rows = pl.ds(pl.multiple_of(to_y * 256, 256), 256)
        left_rows(rows, columns)
        for part in range(HOME_PARTS):

            @pl.loop(0, HOME_WIDE // 256)
            def _(i):
                here = pl.ds(pl.multiple_of(part * HOME_WIDE + i * 256, 256), 256)
                both = product(mixed_hi[rows], mixed_lo[rows], right_hi[:, here], right_lo[:, here])
                done[2 * to_y, :, here] = both[:128]
                done[2 * to_y + 1, :, here] = both[128:]

            for to_a in range(2):
                src, dst, send, recv, device = p_copy(dy, to_a, part)
                if dy == 0:
                    stays = jnp.logical_and(a == k, a == to_a)

                    @pl.when(stays)
                    def _():
                        pltpu.make_async_copy(src, dst, recv).start()

                    @pl.when(jnp.logical_not(stays))
                    def _():
                        remote(src, dst, send, recv, device).start()
                else:
                    remote(src, dst, send, recv, device).start()

    for copy in late:
        copy.wait()
    for dy in (2, 1, 3, 0):
        for t in range(2):
            b = 2 * step(y, dy * (2 * t - 1)) + t
            for part in range(HOME_PARTS):
                columns = pl.ds(part * HOME_WIDE, HOME_WIDE)
                arrived(home_tile.at[b, :, columns], p_recv.at[b, part])

            @pl.loop(0, 8)
            def _(i):
                rows = pl.ds(pl.multiple_of(i * 16, 16), 16)
                precond = home_tile[b, rows]
                variance_next = second_decay * variance_out[b, rows] + (1.0 - second_decay) * precond * precond
                weight_float = weight_out[b, rows].astype(jnp.float32)
                weight_next = weight_float - learn_rate * (
                    precond / (jnp.sqrt(variance_next) + epsilon) + weight_decay * weight_float
                )
                variance_out[b, rows] = variance_next
                weight_out[b, rows] = weight_next.astype(jnp.bfloat16)

    for t in range(2):

        @pl.when(jnp.logical_not(jnp.logical_and(y == home, k == t)))
        def _():
            l1(t).wait_send()

    for i in range(1, 4):
        r1(i).wait_send()

    @pl.when(holder)
    def _():
        for i in range(1, 4):
            for from_y in range(4):
                l2(i, from_y).wait_send()

    for s in range(2):
        for from_y in range(4):
            l3(0, s, from_y).wait_send()
            l3(1, s, from_y).wait_send()
            l4(s, from_y).wait_send()
        r2(s).wait_send()
        r4(s).wait_send()
    for dy in range(4):
        r3(dy).wait_send()
    for dy in range(4):
        for t in range(2):
            sends = [remote(*own_part(dy, t, part)) for part in range(PARTS)]
            sends += [remote(*p_copy(dy, t, part)) for part in range(HOME_PARTS)]
            if dy == 0:

                @pl.when(jnp.logical_not(jnp.logical_and(a == k, k == t)))
                def _():
                    for copy in sends:
                        copy.wait_send()
            else:
                for copy in sends:
                    copy.wait_send()
def store(momentum, variance, weight, momentum_out, variance_out, weight_out, sem):
    copies = [
        pltpu.make_async_copy(src.at[pl.ds(2 * i, 2)], dst.at[pl.ds(2 * i, 2)], sem.at[n, i])
        for i in range(4)
        for n, (src, dst) in enumerate(((momentum, momentum_out), (variance, variance_out), (weight, weight_out)))
    ]
    for copy in copies:
        copy.start()
    for copy in copies:
        copy.wait()


def update(grad, momentum, variance, weight, left, right):
    f32, bf16 = jnp.float32, jnp.bfloat16
    dma = pltpu.SemaphoreType.DMA
    updated = pl.pallas_call(
        kernel,
        out_shape=(
            pltpu.VMEM((8, 128, 1024), f32),
            pltpu.VMEM((8, 128, 1024), f32),
            pltpu.VMEM((8, 128, 1024), bf16),
        ),
        in_specs=[pl.BlockSpec(memory_space=pl.ANY)] * 6,
        out_specs=(pl.BlockSpec(memory_space=pltpu.VMEM),) * 3,
        scratch_shapes=[
            pltpu.VMEM((8, 128, 1024), bf16),
            pltpu.VMEM((8, 128, 1024), f32),
            pltpu.VMEM((8, 128, 1024), f32),
            pltpu.VMEM((2, 32, KEPT * 128), f32),
            pltpu.VMEM((4, 32, KEPT * 128), f32),
            pltpu.VMEM((4, 2, 4, 32, KEPT * 128), f32),
            pltpu.VMEM((4, 2, 2, 2, 32, KEPT * 128), f32),
            pltpu.VMEM((1024, 1024), bf16),
            pltpu.VMEM((1024, 1024), bf16),
            pltpu.VMEM((1024, 1024), bf16),
            pltpu.VMEM((1024, 1024), bf16),
            pltpu.VMEM((1024, WIDE), bf16),
            pltpu.VMEM((1024, WIDE), bf16),
            pltpu.VMEM((1024, 1024), bf16),
            pltpu.VMEM((1024, 1024), bf16),
            pltpu.VMEM((8, 128, 1024), f32),
            dma((2, 8)), dma((2, KEPT)), dma((2,)),
            dma((4, 2, PARTS)), dma((8, PARTS)),
            dma((2,)), dma((4,)), dma((3, 4)), dma((2, 4)), dma((2, 2, 4)), dma((2, 2, 4)), dma((2, 4)), dma((2, 4)),
            dma((4,)), dma((4,)), dma((2,)), dma((2,)), dma((4,)), dma((4,)), dma((2,)), dma((2,)),
            dma((4, 2, HOME_PARTS)), dma((8, HOME_PARTS)),
        ],
        compiler_params=pltpu.CompilerParams(
            collective_id=0, has_side_effects=True, vmem_limit_bytes=48 * 2**20
        ),
        cost_estimate=pl.CostEstimate(flops=3 * 2**32, bytes_accessed=20 * 2**20, transcendentals=0),
    )(grad, momentum, variance, weight, left, right)
    return pl.pallas_call(
        store,
        out_shape=[jax.ShapeDtypeStruct(x.shape, x.dtype) for x in updated],
        in_specs=[pl.BlockSpec(memory_space=pl.ANY)] * 3,
        out_specs=[pl.BlockSpec(memory_space=pl.ANY)] * 3,
        scratch_shapes=[dma((3, 4))],
        compiler_params=pltpu.CompilerParams(vmem_limit_bytes=2**20),
    )(*updated)


def solution(mesh):
    torus = Mesh(mesh.devices.reshape(4, 2, 2, 2, 4), AXES)
    tiles = P(None, ("y", "a"), ("h", "k", "z"))
    in_specs = (
        tiles,
        tiles,
        tiles,
        tiles,
        P(("h", "k"), ("y", "a", "z"), None),
        P(None, "z", ("y", "a", "h", "k"), None),
    )
    return jax.shard_map(
        update, mesh=torus, in_specs=in_specs, out_specs=(tiles, tiles, tiles), check_vma=False
    )
```
